256 devices in a mesh: layer: 4 (over z_hi, core), lat: 64 (over z_lo, x, y).
Axes of the slice: x: 4, y: 4, z: 8 (z_hi: 2, z_lo: 4; z = z_hi * 4 + z_lo), core: 2. Of those that a mesh axis runs over, the one named last changes fastest.
Arguments:
- resid_in: bfloat16 [128, 2, 4, 2304], P('lat', None, 'layer'), may hold values from -6 to 6
- enc_weight: bfloat16 [2, 4, 2304, 8192], P(None, 'layer', None, 'lat'), may hold values from -0.125 to 0.125
- enc_bias: bfloat16 [2, 4, 8192], P(None, 'layer', 'lat'), may hold values from -4 to 4
- dec_weight: bfloat16 [4, 9, 8192, 2304], P('layer', None, 'lat'), may hold values from -0.0625 to 0.0625
- dec_bias: bfloat16 [8, 2304], P('layer'), may hold values from -3 to 3
- act_blocks: int32 [2, 4, 2, 16], P(None, 'layer'), may hold values from 0 to 63, all different within a row
- tile_order: int32 [2], replicated, may hold values from 0 to 1, each once
- targets: bfloat16 [128, 8, 2304], P('lat', 'layer'), may hold values from -6 to 6
Outputs:
- recon_error: bfloat16 [128, 8, 2304], P('lat', 'layer')
- dec_grad: bfloat16 [4, 9, 8192, 2304], P('layer', None, 'lat')
The draws below stay inside these ranges and needn't reach their ends.
Inputs may be any that keep to these rules, and one draw needn't show every extreme that they name: `act_blocks`: each row lists 16 different latent blocks, and every block is listed by some row. `tile_order`: a permutation of the 2 token tiles.
All inputs are finite; a program needn't handle non-finite values.
Results may differ from the reference program's by a relative error of at most 0.0037.
Values may be sent and summed in bfloat16 or wider, within the bound.
No kernel may reach another device: no remote copies, remote signals or barrier semaphores. Data moves between devices by JAX's collectives and lax.ppermute only.
A program may use at most 128 MiB of HBM per device.

```python
import jax
import jax.numpy as jnp
from jax import lax

D = 2304
F = 8192
BLK = 128
KACT = 16
TILE = 64
TOKENS = 128
LAYERS = 8
PAIRS = 9
NTILES = 2
NB = 64
N_LAYER = 4


def steps_of(own_key, extent, cuts, smallest, top_value):
    loudness = 1.0
    for position, blocks in cuts:
        steps = jax.random.uniform(jax.random.fold_in(jax.random.fold_in(own_key, 6), position), (blocks,), jnp.float32, smallest / len(cuts), top_value / len(cuts))
        loudness = loudness * jnp.repeat(jnp.exp(steps), extent[position] // blocks).reshape((-1,) + (1,) * (len(extent) - 1 - position))
    return loudness


def choose_distinct(key, rows, number_of, top, lift):
    ranking = jax.random.permutation(jax.random.fold_in(key, 1), number_of)
    favour = ranking
    for power in range(3):
        favour = favour * favour // number_of
    favour = favour * lift // number_of
    chance = jax.random.randint(jax.random.fold_in(key, 2), (rows, number_of), 0, 4096) + favour
    sure = jax.random.permutation(jax.random.fold_in(key, 3), rows)[jnp.arange(number_of) % rows]
    chance = jnp.where(jnp.arange(rows)[:, None] == sure[None, :], 1 << 14, chance)
    merit = chance * number_of + jnp.arange(number_of)
    return lax.top_k(merit.astype(jnp.int32), top)[1].astype(jnp.int32)


def normal_values(key, shape, scale, bound, cuts=(), kind=jnp.bfloat16):
    loudness = steps_of(key, shape, cuts, -0.22, 0.18) if cuts else 1.0
    entries = jax.random.normal(key, shape, jnp.float32) * scale * loudness
    return jnp.minimum(jnp.maximum(entries, -bound), bound).astype(kind)


def setup_inputs(seed: int = 0) -> dict:
    keys = jax.random.split(jax.random.key(seed), 9)
    resid_in = normal_values(keys[0], (TOKENS, 2, N_LAYER, D), 1.0, 6.0, ((0, 64), (2, 4)))
    enc_weight = normal_values(keys[1], (2, N_LAYER, D, F), D ** -0.5, 0.125, ((1, 4), (3, 64)))
    enc_bias = normal_values(keys[2], (2, N_LAYER, F), 1.0, 4.0, ((1, 4), (2, 64)))
    dec_weight = normal_values(keys[3], (N_LAYER, PAIRS, F, D), F ** -0.5, 0.0625, ((0, 4), (2, 64)))
    dec_bias = normal_values(keys[4], (LAYERS, D), 0.5, 3.0, ((0, 4),))
    act_blocks = choose_distinct(keys[5], 2 * N_LAYER * NTILES, NB, KACT, 2048).reshape((2, N_LAYER, NTILES, KACT))
    tile_order = jax.random.permutation(keys[6], NTILES).astype(jnp.int32)
    targets = normal_values(keys[7], (TOKENS, LAYERS, D), 1.0, 6.0, ((0, 64), (1, 4)))
    return {"resid_in": resid_in, "enc_weight": enc_weight, "enc_bias": enc_bias, "dec_weight": dec_weight, "dec_bias": dec_bias, "act_blocks": act_blocks, "tile_order": tile_order, "targets": targets}


def reference(resid_in, enc_weight, enc_bias, dec_weight, dec_bias, act_blocks, tile_order, targets):
    token_tile = tile_order[jnp.arange(TOKENS, dtype=jnp.int32) // TILE]
    block_of = jnp.arange(F, dtype=jnp.int32) // BLK
    latent_map = {}
    for half_idx in range(2):
        for owner_idx in range(N_LAYER):
            listed = act_blocks[half_idx, owner_idx][token_tile]
            active = jnp.any(listed[:, :, None] == block_of[None, None, :], axis=1)
            pre_act = jnp.dot(resid_in[:, half_idx, owner_idx, :], enc_weight[half_idx, owner_idx],
                              preferred_element_type=jnp.float32) + enc_bias[half_idx, owner_idx].astype(jnp.float32)
            latent_map[(half_idx, owner_idx)] = jnp.where(active, jnp.maximum(pre_act, 0.0), 0.0).astype(jnp.bfloat16)
    slot_table = []
    for owner_idx in range(N_LAYER):
        for slot_idx in range(PAIRS):
            if slot_idx < LAYERS - owner_idx:
                slot_table.append((owner_idx, slot_idx, 0, owner_idx + slot_idx))
            else:
                slot_table.append((owner_idx, slot_idx, 1, slot_idx - 1))
    recon_sum = [jnp.broadcast_to(dec_bias[target_idx].astype(jnp.float32)[None, :], (TOKENS, D))
                 for target_idx in range(LAYERS)]
    for owner_idx, slot_idx, half_idx, target_idx in slot_table:
        recon_sum[target_idx] = recon_sum[target_idx] + jnp.dot(
            latent_map[(half_idx, owner_idx)], dec_weight[owner_idx, slot_idx], preferred_element_type=jnp.float32)
    recon_error = (jnp.stack(recon_sum, axis=1) - targets.astype(jnp.float32)).astype(jnp.bfloat16)
    grad_scale = TOKENS ** -0.5
    grad_list = []
    for owner_idx, slot_idx, half_idx, target_idx in slot_table:
        product = jnp.dot(latent_map[(half_idx, owner_idx)].T, recon_error[:, target_idx, :],
                          preferred_element_type=jnp.float32)
        grad_list.append((product * grad_scale).astype(jnp.bfloat16))
    dec_grad = jnp.stack(grad_list).reshape(N_LAYER, PAIRS, F, D)
    return (recon_error, dec_grad)
```

```python
import functools

import jax
import jax.numpy as jnp
from jax import lax
from jax.experimental import pallas as pl
from jax.experimental.pallas import tpu as pltpu
from jax.sharding import Mesh
from jax.sharding import PartitionSpec as P

BLK = 128
D = 2304
DC = 768
PAIRS = 9
LAYERS = 8
SEND = 2.0**-5
VMEM = 48 * 1024 * 1024
XY = ("x", "y")
Z = ("zh", "zl")
LAT = ("zl", "x", "y")
LAYER = ("zh", "co")


def enc_kernel(pos, act, order, rows, weight, bias, out):
    lat_index = pos[2]
    g = rows[...]
    tile_row = lax.broadcasted_iota(jnp.int32, (256, BLK), 0) // 8 % 2
    q = lax.broadcasted_iota(jnp.int32, (256, 256), 0)
    c = lax.broadcasted_iota(jnp.int32, (256, 256), 1)
    for h in range(2):
        pre = jnp.dot(g, weight[h], preferred_element_type=jnp.float32)
        pre = pre + bias[h].astype(jnp.float32)
        hits = []
        for tile in range(2):
            hit = jnp.int32(0)
            for j in range(16):
                hit = hit | (act[h, order[tile], j] == lat_index).astype(jnp.int32)
            hits.append(hit)
        on = jnp.where(tile_row == 0, hits[0], hits[1]) > 0
        lat = jnp.where(on, jnp.maximum(pre, 0.0), 0.0).astype(jnp.bfloat16)
        for tt in range(2):
            pick = (q // 2 == c // 2) & (q % 2 == tt) & (c % 2 == h)
            out[h, tt] = jnp.dot(
                pick.astype(jnp.bfloat16), lat, preferred_element_type=jnp.float32
            ).astype(jnp.bfloat16)


def encode(pos, act, order, rows, weight, bias):
    return pl.pallas_call(
        enc_kernel,
        grid_spec=pltpu.PrefetchScalarGridSpec(
            num_scalar_prefetch=3,
            grid=(1,),
            in_specs=[
                pl.BlockSpec((256, D), lambda *_: (0, 0)),
                pl.BlockSpec((2, D, BLK), lambda *_: (0, 0, 0)),
                pl.BlockSpec((2, 1, BLK), lambda *_: (0, 0, 0)),
            ],
            out_specs=pl.BlockSpec((2, 2, 256, BLK), lambda *_: (0, 0, 0, 0)),
        ),
        out_shape=jax.ShapeDtypeStruct((2, 2, 256, BLK), jnp.bfloat16),
        compiler_params=pltpu.CompilerParams(vmem_limit_bytes=VMEM),
        name="encode",
    )(pos, act, order, rows, weight, bias)


def dec_kernel(mine, pos, lat, w00, w01, w10, w11, out):
    owner = pos[0]
    core = pos[1] if mine else 1 - pos[1]
    first = 2 * (2 * pl.program_id(1) + core)

    def half(h, weights):
        cols = []
        for tt in range(2):
            target = first + tt
            valid = (target >= owner) if h == 0 else (target + 1 >= LAYERS - owner)
            cols.append(lat[h, tt] * valid.astype(jnp.bfloat16))
        return jnp.dot(
            jnp.concatenate(cols, axis=1),
            jnp.concatenate([w[0] for w in weights], axis=0),
            preferred_element_type=jnp.float32,
        )

    total = (half(0, (w00, w01)) + half(1, (w10, w11))) * SEND
    out[...] = total.reshape(16, 1, 16, DC)


def decode(mine, pos, lat, weight):
    def slot(h, tt):
        def index(d, zh, pos):
            core = pos[1] if mine else 1 - pos[1]
            target = 2 * (2 * zh + core) + tt
            if h == 0:
                k = jnp.maximum(target - pos[0], 0)
            else:
                k = jnp.maximum(target + 1, LAYERS - pos[0])
            return (k, 0, d)

        return pl.BlockSpec((1, BLK, DC), index)

    piece = pl.BlockSpec((16, 1, 16, DC), lambda d, zh, pos: (0, zh, 0, d))
    return pl.pallas_call(
        functools.partial(dec_kernel, mine),
        grid_spec=pltpu.PrefetchScalarGridSpec(
            num_scalar_prefetch=1,
            grid=(D // DC, 2),
            in_specs=[pl.BlockSpec((2, 2, 256, BLK), lambda *_: (0, 0, 0, 0))]
            + [slot(0, 0), slot(0, 1), slot(1, 0), slot(1, 1)],
            out_specs=piece,
        ),
        out_shape=jax.ShapeDtypeStruct((16, 2, 16, D), jnp.float32),
        compiler_params=pltpu.CompilerParams(vmem_limit_bytes=VMEM),
        name="decode",
    )(pos, lat, weight, weight, weight, weight)


def grad_kernel(pos, lat, own, other, out):
    owner = pos[0]
    k = pl.program_id(1)
    late = (k >= LAYERS - owner).astype(jnp.int32)
    target = jnp.where(late == 1, k - 1, owner + k)
    pair = target // 2
    lhs = lat[late, target % 2]

    def put(err):
        rows = err[:, pl.ds(pair // 2, 1)].reshape(256, DC)
        total = lax.dot_general(
            lhs, rows, (((0,), (0,)), ((), ())), preferred_element_type=jnp.float32
        )
        out[0] = (total * (BLK**-0.5)).astype(jnp.bfloat16)

    is_own = pair % 2 == pos[1]

    @pl.when(is_own)
    def _():
        put(own)

    @pl.when(jnp.logical_not(is_own))
    def _():
        put(other)


def gradients(pos, lat, own, other):
    errs = pl.BlockSpec((16, 2, 16, DC), lambda d, k, pos: (0, 0, 0, d))
    return pl.pallas_call(
        grad_kernel,
        grid_spec=pltpu.PrefetchScalarGridSpec(
            num_scalar_prefetch=1,
            grid=(D // DC, PAIRS),
            in_specs=[pl.BlockSpec((2, 2, 256, BLK), lambda *_: (0, 0, 0, 0)), errs, errs],
            out_specs=pl.BlockSpec((1, BLK, DC), lambda d, k, pos: (k, 0, d)),
        ),
        out_shape=jax.ShapeDtypeStruct((PAIRS, BLK, D), jnp.bfloat16),
        compiler_params=pltpu.CompilerParams(vmem_limit_bytes=VMEM),
        name="gradients",
    )(pos, lat, own, other)


def spread(block, axes, n):
    copies = jnp.broadcast_to(block[None], (n,) + block.shape)
    return lax.all_to_all(copies, axes, 0, 0, tiled=True)


def local(resid_in, enc_weight, enc_bias, dec_weight, dec_bias, act_blocks, tile_order, targets):
    pos = jnp.stack([lax.axis_index(LAYER), lax.axis_index("co"), lax.axis_index(LAT)]).astype(jnp.int32)
    swap = [(0, 1), (1, 0)]
    rows = spread(resid_in.reshape(4, D), "zl", 4).reshape(16, D)
    rows = spread(rows, XY, 16).reshape(256, D)
    lat = encode(pos, act_blocks[:, 0], tile_order, rows, enc_weight[:, 0], enc_bias)
    away = decode(False, pos, lat, dec_weight[0])
    received = lax.ppermute(away.astype(jnp.float16), "co", swap)
    partial = decode(True, pos, lat, dec_weight[0]) + received.astype(jnp.float32)
    parts = lax.all_to_all(partial.astype(jnp.float16).reshape(16, 32, D), XY, 0, 0, tiled=True)
    column = jnp.sum(parts.astype(jnp.float32), axis=0).reshape(8, 4, D)
    column = lax.all_to_all(column, Z, 0, 0, tiled=True)
    recon = jnp.sum(column, axis=0).reshape(2, 2, D) * (1.0 / SEND)
    recon_error = (
        recon + dec_bias.astype(jnp.float32)[None] - targets.astype(jnp.float32)
    ).astype(jnp.bfloat16)
    errs = spread(recon_error.reshape(4, D), Z, 8).reshape(32, D)
    own = spread(errs, XY, 16).reshape(16, 2, 16, D)
    other = lax.ppermute(own, "co", swap)
    return (recon_error, gradients(pos, lat, own, other)[None])


def solution(mesh):
    fine = Mesh(mesh.devices.reshape(2, 2, 4, 4, 4), ("zh", "co", "zl", "x", "y"))
    return jax.shard_map(
        local,
        mesh=fine,
        in_specs=(
            P(LAT, None, LAYER, None),
            P(None, LAYER, None, LAT),
            P(None, LAYER, LAT),
            P(LAYER, None, LAT, None),
            P(LAYER, None),
            P(None, LAYER, None, None),
            P(),
            P(LAT, LAYER, None),
        ),
        out_specs=(P(LAT, LAYER, None), P(LAYER, None, LAT, None)),
        check_vma=False,
    )
```

```python
import functools

import jax
import jax.numpy as jnp
import numpy as np
from jax import lax
from jax.experimental import pallas as pl
from jax.experimental.pallas import tpu as pltpu
from jax.sharding import Mesh
from jax.sharding import PartitionSpec as P

BLK = 128
D = 2304
DC = 768
PAIRS = 9
LAYERS = 8
SEND = 2.0**-5
VMEM = 24 * 1024 * 1024
XY = ("x", "y")
Z = ("zh", "zl")
LAT = ("zl", "x", "y")
LAYER = ("zh", "co")


def enc_kernel(pos, act, order, rows, weight, bias, out):
    lat_index = pos[2]
    g = rows[...]
    tile_row = lax.broadcasted_iota(jnp.int32, (256, BLK), 0) // 8 % 2
    q = lax.broadcasted_iota(jnp.int32, (256, 256), 0)
    c = lax.broadcasted_iota(jnp.int32, (256, 256), 1)
    for h in range(2):
        pre = jnp.dot(g, weight[h], preferred_element_type=jnp.float32)
        pre = pre + bias[h].astype(jnp.float32)
        hits = []
        for tile in range(2):
            hit = jnp.int32(0)
            for j in range(16):
                hit = hit | (act[h, order[tile], j] == lat_index).astype(jnp.int32)
            hits.append(hit)
        on = jnp.where(tile_row == 0, hits[0], hits[1]) > 0
        lat = jnp.where(on, jnp.maximum(pre, 0.0), 0.0).astype(jnp.bfloat16)
        for tt in range(2):
            pick = (q // 2 == c // 2) & (q % 2 == tt) & (c % 2 == h)
            out[h, tt] = jnp.dot(
                pick.astype(jnp.bfloat16), lat, preferred_element_type=jnp.float32
            ).astype(jnp.bfloat16)


def encode(pos, act, order, rows, weight, bias):
    return pl.pallas_call(
        enc_kernel,
        grid_spec=pltpu.PrefetchScalarGridSpec(
            num_scalar_prefetch=3,
            grid=(1,),
            in_specs=[
                pl.BlockSpec((256, D), lambda *_: (0, 0)),
                pl.BlockSpec((2, D, BLK), lambda *_: (0, 0, 0)),
                pl.BlockSpec((2, 1, BLK), lambda *_: (0, 0, 0)),
            ],
            out_specs=pl.BlockSpec((2, 2, 256, BLK), lambda *_: (0, 0, 0, 0)),
        ),
        out_shape=jax.ShapeDtypeStruct((2, 2, 256, BLK), jnp.bfloat16),
        compiler_params=pltpu.CompilerParams(vmem_limit_bytes=VMEM),
        name="encode",
    )(pos, act, order, rows, weight, bias)


def dec_kernel(mine, pos, lat, weight, out):
    owner = pos[0]
    core = pos[1] if mine else 1 - pos[1]
    for zh in range(2):
        first = 2 * (2 * zh + core)
        left, slots = [], []
        for h in range(2):
            cols = []
            for tt in range(2):
                target = first + tt
                if h == 0:
                    valid = target >= owner
                    slots.append(jnp.maximum(target - owner, 0))
                else:
                    valid = target + 1 >= LAYERS - owner
                    slots.append(jnp.maximum(target + 1, LAYERS - owner))
                cols.append(lat[h, tt] * valid.astype(jnp.bfloat16))
            left.append(jnp.concatenate(cols, axis=1))
        for d in range(0, D, DC):
            total = jnp.zeros((256, DC), jnp.float32)
            for h in range(2):
                right = [weight[slots[2 * h + tt], :, d : d + DC] for tt in range(2)]
                total += jnp.dot(
                    left[h], jnp.concatenate(right, axis=0), preferred_element_type=jnp.float32
                )
            out[:, zh, :, d : d + DC] = (total * SEND).reshape(16, 16, DC)


def decode(mine, pos, lat, weight):
    return pl.pallas_call(
        functools.partial(dec_kernel, mine),
        in_specs=[
            pl.BlockSpec(memory_space=pltpu.SMEM),
            pl.BlockSpec(memory_space=pltpu.VMEM),
            pl.BlockSpec(memory_space=pltpu.VMEM),
        ],
        out_specs=pl.BlockSpec(memory_space=pltpu.VMEM),
        out_shape=jax.ShapeDtypeStruct((16, 2, 16, D), jnp.float32),
        cost_estimate=pl.CostEstimate(
            flops=4 * 2 * 256 * 256 * D, bytes_accessed=10 * 2**20, transcendentals=0
        ),
        compiler_params=pltpu.CompilerParams(vmem_limit_bytes=VMEM),
        name="decode",
    )(pos, lat, weight)


def grad_kernel(which, pos, table, lat, errs, *rest):
    out = rest[-1]
    entry = ((pos[0] * 2 + which) * 6 + pl.program_id(0)) * 4
    rows = errs[:, pl.ds(table[entry + 2], 1)].reshape(256, D)
    total = lax.dot_general(
        lat[table[entry + 1], table[entry + 3]],
        rows,
        (((0,), (0,)), ((), ())),
        preferred_element_type=jnp.float32,
    )
    out[0] = (total * (BLK**-0.5)).astype(jnp.bfloat16)


def gradients(which, pos, lat, errs, *before):
    def slot(j, pos, table):
        return (table[((pos[0] * 2 + which) * 6 + j) * 4], 0, 0)

    return pl.pallas_call(
        functools.partial(grad_kernel, which),
        grid_spec=pltpu.PrefetchScalarGridSpec(
            num_scalar_prefetch=2,
            grid=(6,),
            in_specs=[
                pl.BlockSpec(memory_space=pltpu.VMEM),
                pl.BlockSpec(memory_space=pltpu.VMEM),
            ]
            + [pl.BlockSpec(memory_space=pl.ANY)] * len(before),
            out_specs=pl.BlockSpec((1, BLK, D), slot),
        ),
        out_shape=jax.ShapeDtypeStruct((PAIRS, BLK, D), jnp.bfloat16),
        input_output_aliases={4: 0} if before else {},
        cost_estimate=pl.CostEstimate(
            flops=6 * 2 * BLK * 256 * D, bytes_accessed=10 * 2**20, transcendentals=0
        ),
        compiler_params=pltpu.CompilerParams(vmem_limit_bytes=VMEM),
        name="gradients",
    )(pos, jnp.asarray(slot_table()), lat, errs, *before)


def slot_table():
    table = np.zeros((4, 2, 6, 4), np.int32)
    for owner in range(4):
        for which in range(2):
            entries = []
            for k in range(PAIRS):
                late = int(k >= LAYERS - owner)
                target = k - 1 if late else owner + k
                if (target // 2 % 2 == owner % 2) == (which == 0):
                    entries.append((k, late, target // 4, target % 2))
            table[owner, which] = (entries + [entries[-1]] * 6)[:6]
    return table.reshape(-1)


def spread(block, axes, n):
    copies = jnp.broadcast_to(block[None], (n,) + block.shape)
    return lax.all_to_all(copies, axes, 0, 0, tiled=True)


def local(resid_in, enc_weight, enc_bias, dec_weight, dec_bias, act_blocks, tile_order, targets):
    pos = jnp.stack([lax.axis_index(LAYER), lax.axis_index("co"), lax.axis_index(LAT)]).astype(jnp.int32)
    swap = [(0, 1), (1, 0)]
    rows = spread(resid_in.reshape(4, D), "zl", 4).reshape(16, D)
    rows = spread(rows, XY, 16).reshape(256, D)
    lat = encode(pos, act_blocks[:, 0], tile_order, rows, enc_weight[:, 0], enc_bias)
    away = decode(False, pos, lat, dec_weight[0])
    received = lax.ppermute(away.astype(jnp.float16), "co", swap)
    partial = decode(True, pos, lat, dec_weight[0]) + received.astype(jnp.float32)
    parts = lax.all_to_all(partial.astype(jnp.float16).reshape(16, 32, D), XY, 0, 0, tiled=True)
    column = jnp.sum(parts.astype(jnp.float32), axis=0).astype(jnp.float16).reshape(8, 4, D)
    column = lax.all_to_all(column, Z, 0, 0, tiled=True).astype(jnp.float32)
    recon = jnp.sum(column, axis=0).reshape(2, 2, D) * (1.0 / SEND)
    recon_error = (
        recon + dec_bias.astype(jnp.float32)[None] - targets.astype(jnp.float32)
    ).astype(jnp.bfloat16)
    errs = spread(recon_error.reshape(4, D), Z, 8).reshape(32, D)
    own = spread(errs, XY, 16).reshape(16, 2, 16, D)
    other = lax.ppermute(own, "co", swap)
    dec_grad = gradients(0, pos, lat, own)
    dec_grad = gradients(1, pos, lat, other, dec_grad)
    return (recon_error, dec_grad[None])


def solution(mesh):
    fine = Mesh(mesh.devices.reshape(2, 2, 4, 4, 4), ("zh", "co", "zl", "x", "y"))
    return jax.shard_map(
        local,
        mesh=fine,
        in_specs=(
            P(LAT, None, LAYER, None),
            P(None, LAYER, None, LAT),
            P(None, LAYER, LAT),
            P(LAYER, None, LAT, None),
            P(LAYER, None),
            P(None, LAYER, None, None),
            P(),
            P(LAT, LAYER, None),
        ),
        out_specs=(P(LAT, LAYER, None), P(LAYER, None, LAT, None)),
        check_vma=False,
    )
```

```python
import functools

import jax
import jax.numpy as jnp
from jax import lax
from jax.experimental import pallas as pl
from jax.experimental.pallas import tpu as pltpu
from jax.sharding import Mesh
from jax.sharding import PartitionSpec as P

BLK = 128
D = 2304
DC = 768
PAIRS = 9
LAYERS = 8
SEND = 2.0**-5
VMEM = 24 * 1024 * 1024
LARGE = 44 * 1024 * 1024
Z = ("zh", "zl")
LAT = ("zl", "x", "y")
LAYER = ("zh", "co")


def product(zh, core, owner, lat, weight, put):
    first = 2 * (2 * zh + core)
    left = []
    for h in range(2):
        cols = []
        for tt in range(2):
            target = first + tt
            valid = (target >= owner) if h == 0 else (target + 1 >= LAYERS - owner)
            cols.append(lat[h, tt] * valid.astype(jnp.bfloat16))
        left.append(jnp.concatenate(cols, axis=1))
    for d in range(0, D, DC):
        total = jnp.zeros((256, DC), jnp.float32)
        for h in range(2):
            right = [weight[4 * zh + 2 * h + tt, :, d : d + DC] for tt in range(2)]
            total += jnp.dot(
                left[h], jnp.concatenate(right, axis=0), preferred_element_type=jnp.float32
            )
        put(d, (total * SEND).reshape(16, 16, DC))


def decoder_slots(zh, core, owner):
    slots = []
    for h in range(2):
        for tt in range(2):
            target = 2 * (2 * zh + core) + tt
            if h == 0:
                slots.append(jnp.maximum(target - owner, 0))
            else:
                slots.append(jnp.maximum(target + 1, LAYERS - owner))
    return slots


def fetch(zh, core, owner, weight, held, sems):
    copies = []
    for j, slot in enumerate(decoder_slots(zh, core, owner)):
        j += 4 * zh
        copies.append(pltpu.make_async_copy(weight.at[slot], held.at[j], sems.at[j]))
    return copies


def decode_pairs(core, owner, lat, held, copies, out):
    for zh in range(2):
        for copy in copies[zh]:
            copy.wait()

        def put(d, block):
            out[:, zh, :, d : d + DC] = block

        product(zh, core, owner, lat, held, put)


def away_kernel(pos, act, order, enc, bias, dec, g0, g1, g2, g3, lat, out, enc_held, held, enc_sems, sems):
    owner, core, lat_index, zl = (pos[j] for j in range(4))
    enc_copies = [pltpu.make_async_copy(enc.at[h], enc_held.at[h], enc_sems.at[h]) for h in range(2)]
    dec_copies = [fetch(zh, 1 - core, owner, dec, held, sems) for zh in range(2)]
    for copy in enc_copies + dec_copies[0] + dec_copies[1]:
        copy.start()
    g = jnp.concatenate([g0[...], g1[...], g2[...], g3[...]], axis=0)
    tile_row = (lax.broadcasted_iota(jnp.int32, (256, BLK), 0) // 4 + zl) % 4 // 2
    q = lax.broadcasted_iota(jnp.int32, (256, 256), 0)
    c = lax.broadcasted_iota(jnp.int32, (256, 256), 1)
    same = (q // 4 % 4 == (c // 4 + zl) % 4) & (q // 2 % 2 == c // 2 % 2)
    own = same & (q // 16 == c // 16)
    other = same & (c // 64 == q // 16 % 4) & (c // 16 % 4 == q // 64)
    for h in range(2):
        enc_copies[h].wait()
        pre = jnp.dot(g, enc_held[h], preferred_element_type=jnp.float32)
        pre = pre + bias[0, h : h + 1].astype(jnp.float32)
        hits = []
        for tile in range(2):
            hit = jnp.int32(0)
            for j in range(16):
                hit = hit | (act[h, order[tile], j] == lat_index).astype(jnp.int32)
            hits.append(hit)
        on = jnp.where(tile_row == 0, hits[0], hits[1]) > 0
        value = jnp.where(on, jnp.maximum(pre, 0.0), 0.0).astype(jnp.bfloat16)
        for tt in range(2):
            half = (q % 2 == tt) & (c % 2 == h)
            for which, place in enumerate((own, other)):
                lat[which, h, tt] = jnp.dot(
                    (place & half).astype(jnp.bfloat16), value, preferred_element_type=jnp.float32
                ).astype(jnp.bfloat16)
    decode_pairs(1 - core, owner, lat.at[1], held, dec_copies, out)


def mine_kernel(pos, lat, dec, dec_bias, targets, out, base, held, sems):
    owner, core = pos[0], pos[1]
    copies = [fetch(zh, core, owner, dec, held, sems) for zh in range(2)]
    for copy in copies[0] + copies[1]:
        copy.start()
    for r in range(2):
        for tt in range(2):
            row = dec_bias[tt : tt + 1].astype(jnp.float32) - targets[r, tt : tt + 1].astype(jnp.float32)
            base[2 * r + tt : 2 * r + tt + 1] = row
    decode_pairs(core, owner, lat.at[0], held, copies, out)


SM = pl.BlockSpec(memory_space=pltpu.SMEM)
VM = pl.BlockSpec(memory_space=pltpu.VMEM)
ANY = pl.BlockSpec(memory_space=pltpu.HBM)
PARTIAL = jax.ShapeDtypeStruct((16, 2, 16, D), jnp.float32)


HELD = [pltpu.VMEM((8, BLK, D), jnp.bfloat16)]
SEMS = [pltpu.SemaphoreType.DMA((8,))]


def away(pos, act, order, enc, bias, dec, rows):
    return pl.pallas_call(
        away_kernel,
        in_specs=[SM, SM, SM, ANY, VM, ANY, VM, VM, VM, VM],
        out_specs=(VM, VM),
        out_shape=(jax.ShapeDtypeStruct((2, 2, 2, 256, BLK), jnp.bfloat16), PARTIAL),
        scratch_shapes=[pltpu.VMEM((2, D, BLK), jnp.bfloat16)]
        + HELD
        + [pltpu.SemaphoreType.DMA((2,))]
        + SEMS,
        cost_estimate=pl.CostEstimate(
            flops=6 * 2 * 256 * 256 * D, bytes_accessed=12 * 2**20, transcendentals=0
        ),
        compiler_params=pltpu.CompilerParams(vmem_limit_bytes=LARGE),
        name="encode_and_decode_away",
    )(pos, act, order, enc, bias, dec, *rows)


def mine(pos, lat, dec, dec_bias, targets):
    return pl.pallas_call(
        mine_kernel,
        in_specs=[SM, VM, ANY, VM, VM],
        out_specs=(VM, VM),
        out_shape=(PARTIAL, jax.ShapeDtypeStruct((4, D), jnp.float32)),
        scratch_shapes=HELD + SEMS,
        cost_estimate=pl.CostEstimate(
            flops=4 * 2 * 256 * 256 * D, bytes_accessed=10 * 2**20, transcendentals=0
        ),
        compiler_params=pltpu.CompilerParams(vmem_limit_bytes=LARGE),
        name="decode_mine",
    )(pos, lat, dec, dec_bias, targets)


def grad_kernel(which, pos, lat, errs, *rest):
    out, held, sems = rest[-3:]
    owner = pos[0]
    core = pos[1] if which == 0 else 1 - pos[1]
    place = pos[4 + which]
    writes = []
    for zh in range(2):
        lhs = jnp.concatenate([lat[which, h, tt] for h in range(2) for tt in range(2)], axis=1)
        for d in range(0, D, DC):
            rows = [errs[(place + k) % 4, :, zh, :, d : d + DC].reshape(64, DC) for k in range(4)]
            total = lax.dot_general(
                lhs,
                jnp.concatenate(rows, axis=0),
                (((0,), (0,)), ((), ())),
                preferred_element_type=jnp.float32,
            )
            total = (total * (BLK**-0.5)).astype(jnp.bfloat16).reshape(4, BLK, DC)
            held[4 * zh : 4 * zh + 4, :, d : d + DC] = total
        for j, slot in enumerate(decoder_slots(zh, core, owner)):
            target = 2 * (2 * zh + core) + j % 2
            valid = (target >= owner) if j < 2 else (target + 1 >= LAYERS - owner)
            j += 4 * zh
            copy = pltpu.make_async_copy(held.at[j], out.at[slot], sems.at[j])
            pl.when(valid)(copy.start)
            writes.append((valid, copy))
    for valid, copy in writes:
        pl.when(valid)(copy.wait)


def gradients(which, pos, lat, errs, *before):
    return pl.pallas_call(
        functools.partial(grad_kernel, which),
        in_specs=[SM, VM, VM] + [ANY] * len(before),
        out_specs=ANY,
        out_shape=jax.ShapeDtypeStruct((PAIRS, BLK, D), jnp.bfloat16),
        scratch_shapes=HELD + SEMS,
        input_output_aliases={3: 0} if before else {},
        cost_estimate=pl.CostEstimate(
            flops=4 * 2 * 256 * 256 * D, bytes_accessed=8 * 2**20, transcendentals=0
        ),
        compiler_params=pltpu.CompilerParams(vmem_limit_bytes=VMEM),
        name="gradients",
    )(pos, lat, errs, *before)


ALL = ("zh", "co", "zl", "x", "y")


def lines(wide):
    groups = []
    for outer in range(16):
        for other in range(4):
            along_x = (outer // 4 % 2 == 0) == wide
            groups.append(
                [outer * 16 + (k * 4 + other if along_x else other * 4 + k) for k in range(4)]
            )
    return groups


def shift(block, groups, k):
    perm = [(line[i], line[(i + k) % 4]) for line in groups for i in range(4)]
    return lax.ppermute(block, ALL, perm)


def gather4(block, groups):
    return [block] + [shift(block, groups, -k) for k in (1, 2, 3)]


def reduce4(pieces, groups):
    total = pieces[0].astype(jnp.float32)
    for k in (1, 2, 3):
        total = total + shift(pieces[k], groups, k).astype(jnp.float32)
    return total


def local(resid_in, enc_weight, enc_bias, dec_weight, dec_bias, act_blocks, tile_order, targets):
    core, x, y = lax.axis_index("co"), lax.axis_index("x"), lax.axis_index("y")
    at_wide, at_narrow = jnp.where(core == 0, x, y), jnp.where(core == 0, y, x)
    pos = [lax.axis_index(LAYER), core, lax.axis_index(LAT), lax.axis_index("zl"), at_wide, at_narrow]
    pos = jnp.stack(pos).astype(jnp.int32)
    swap = [(0, 1), (1, 0)]
    wide, narrow = lines(True), lines(False)
    z_lines = [[o // 16 * 64 + k * 16 + o % 16 for k in range(4)] for o in range(64)]
    rows = jnp.concatenate(gather4(resid_in.reshape(4, D), z_lines))
    rows = gather4(jnp.concatenate(gather4(rows, narrow)), wide)
    bias = jnp.swapaxes(enc_bias, 0, 1)
    lat, sent = away(pos, act_blocks[:, 0], tile_order, enc_weight[:, 0], bias, dec_weight[0], rows)
    received = lax.ppermute(sent.astype(jnp.float16), "co", swap)
    partial, base = mine(pos, lat, dec_weight[0], dec_bias, targets)
    partial = (partial + received.astype(jnp.float32)).astype(jnp.float16).reshape(4, 128, D)
    partial = reduce4([partial[k] for k in range(4)], wide).astype(jnp.float16).reshape(4, 32, D)
    column = reduce4([partial[k] for k in range(4)], narrow).astype(jnp.float16).reshape(8, 4, D)
    column = lax.all_to_all(column, Z, 0, 0, tiled=True).astype(jnp.float32)
    errs = (jnp.sum(column, axis=0) * (1.0 / SEND) + base).astype(jnp.bfloat16)
    recon_error = errs.reshape(2, 2, D)
    errs = lax.all_to_all(jnp.broadcast_to(errs[None], (8, 4, D)), Z, 0, 0, tiled=True)
    errs = jnp.concatenate(gather4(errs.reshape(32, D), narrow))
    own = jnp.broadcast_to(errs[None], (4, 128, D))
    own = lax.all_to_all(own, ALL, 0, 0, axis_index_groups=wide, tiled=True).reshape(4, 4, 2, 16, D)
    other = lax.ppermute(own, "co", swap)
    dec_grad = gradients(0, pos, lat, own)
    dec_grad = gradients(1, pos, lat, other, dec_grad)
    return (recon_error, dec_grad[None])


def solution(mesh):
    fine = Mesh(mesh.devices.reshape(2, 2, 4, 4, 4), ALL)
    return jax.shard_map(
        local,
        mesh=fine,
        in_specs=(
            P(LAT, None, LAYER, None),
            P(None, LAYER, None, LAT),
            P(None, LAYER, LAT),
            P(LAYER, None, LAT, None),
            P(LAYER, None),
            P(None, LAYER, None, None),
            P(),
            P(LAT, LAYER, None),
        ),
        out_specs=(P(LAT, LAYER, None), P(LAYER, None, LAT, None)),
        check_vma=False,
    )
```

```python
import functools

import jax
import jax.numpy as jnp
from jax import lax
from jax.experimental import pallas as pl
from jax.experimental.pallas import tpu as pltpu
from jax.sharding import Mesh
from jax.sharding import PartitionSpec as P

BLK = 128
D = 2304
DC = 768
PAIRS = 9
LAYERS = 8
SEND = 2.0**-5
VMEM = 14 * 1024 * 1024
LARGE = 44 * 1024 * 1024
Z = ("zh", "zl")
LAT = ("zl", "x", "y")
LAYER = ("zh", "co")


def product(zh, core, owner, lat, weight, put):
    first = 2 * (2 * zh + core)
    late = first + 2 >= LAYERS - owner

    def halves(count):
        left = []
        for h in range(count):
            cols = []
            for tt in range(2):
                target = first + tt
                valid = (target >= owner) if h == 0 else (target + 1 >= LAYERS - owner)
                cols.append(lat[h, tt] * valid.astype(jnp.bfloat16))
            left.append(jnp.concatenate(cols, axis=1))
        for d in range(0, D, DC):
            total = jnp.zeros((256, DC), jnp.float32)
            for h in range(count):
                right = [weight[4 * zh + 2 * h + tt, :, d : d + DC] for tt in range(2)]
                total += jnp.dot(
                    left[h], jnp.concatenate(right, axis=0), preferred_element_type=jnp.float32
                )
            put(d, (total * SEND).reshape(16, 16, DC))

    pl.when(late)(lambda: halves(2))
    pl.when(jnp.logical_not(late))(lambda: halves(1))


def decoder_slots(zh, core, owner):
    slots = []
    for h in range(2):
        for tt in range(2):
            target = 2 * (2 * zh + core) + tt
            if h == 0:
                slots.append(jnp.maximum(target - owner, 0))
            else:
                slots.append(jnp.maximum(target + 1, LAYERS - owner))
    return slots


def fetch(zh, core, owner, weight, held, sems):
    copies = []
    for j, slot in enumerate(decoder_slots(zh, core, owner)):
        j += 4 * zh
        copies.append(pltpu.make_async_copy(weight.at[slot], held.at[j], sems.at[j]))
    return copies


def decode_pairs(core, owner, lat, held, copies, out):
    for zh in range(2):
        for copy in copies[zh]:
            copy.wait()

        def put(d, block):
            out[:, zh, :, d : d + DC] = block

        product(zh, core, owner, lat, held, put)


def away_kernel(pos, enc, bias, dec, g0, g1, g2, g3, lat, out, enc_held, held, enc_sems, sems):
    owner, core, zl = (pos[j] for j in range(3))
    enc_copies = [pltpu.make_async_copy(enc.at[h], enc_held.at[h], enc_sems.at[h]) for h in range(2)]
    dec_copies = [fetch(zh, 1 - core, owner, dec, held, sems) for zh in range(2)]
    for copy in enc_copies + dec_copies[0] + dec_copies[1]:
        copy.start()
    g = jnp.concatenate([g0[...], g1[...], g2[...], g3[...]], axis=0)
    tile_row = (lax.broadcasted_iota(jnp.int32, (256, BLK), 0) // 4 + zl) % 4 // 2
    q = lax.broadcasted_iota(jnp.int32, (256, 256), 0)
    c = lax.broadcasted_iota(jnp.int32, (256, 256), 1)
    same = (q // 4 % 4 == (c // 4 + zl) % 4) & (q // 2 % 2 == c // 2 % 2)
    own = same & (q // 16 == c // 16)
    other = same & (c // 64 == q // 16 % 4) & (c // 16 % 4 == q // 64)
    for h in range(2):
        enc_copies[h].wait()
        pre = jnp.dot(g, enc_held[h], preferred_element_type=jnp.float32)
        pre = pre + bias[h : h + 1]
        on = jnp.where(tile_row == 0, pos[5 + 2 * h], pos[6 + 2 * h]) > 0
        value = jnp.where(on, jnp.maximum(pre, 0.0), 0.0).astype(jnp.bfloat16)
        for tt in range(2):
            half = (q % 2 == tt) & (c % 2 == h)
            for which, place in enumerate((own, other)):
                lat[which, h, tt] = jnp.dot(
                    (place & half).astype(jnp.bfloat16), value, preferred_element_type=jnp.float32
                ).astype(jnp.bfloat16)
    decode_pairs(1 - core, owner, lat.at[1], held, dec_copies, out)


def mine_kernel(pos, lat, dec, dec_bias, targets, out, base, held, sems):
    owner, core = pos[0], pos[1]
    copies = [fetch(zh, core, owner, dec, held, sems) for zh in range(2)]
    for copy in copies[0] + copies[1]:
        copy.start()
    for r in range(2):
        for tt in range(2):
            row = dec_bias[tt : tt + 1].astype(jnp.float32) - targets[r, tt : tt + 1].astype(jnp.float32)
            base[2 * r + tt : 2 * r + tt + 1] = row
    decode_pairs(core, owner, lat.at[0], held, copies, out)


SM = pl.BlockSpec(memory_space=pltpu.SMEM)
VM = pl.BlockSpec(memory_space=pltpu.VMEM)
ANY = pl.BlockSpec(memory_space=pltpu.HBM)
PARTIAL = jax.ShapeDtypeStruct((16, 2, 16, D), jnp.float32)


HELD = [pltpu.VMEM((8, BLK, D), jnp.bfloat16)]
SEMS = [pltpu.SemaphoreType.DMA((8,))]


def away(pos, enc, bias, dec, rows):
    return pl.pallas_call(
        away_kernel,
        in_specs=[SM, ANY, VM, ANY, VM, VM, VM, VM],
        out_specs=(VM, VM),
        out_shape=(jax.ShapeDtypeStruct((2, 2, 2, 256, BLK), jnp.bfloat16), PARTIAL),
        scratch_shapes=[pltpu.VMEM((2, D, BLK), jnp.bfloat16)]
        + HELD
        + [pltpu.SemaphoreType.DMA((2,))]
        + SEMS,
        cost_estimate=pl.CostEstimate(
            flops=6 * 2 * 256 * 256 * D, bytes_accessed=12 * 2**20, transcendentals=0
        ),
        compiler_params=pltpu.CompilerParams(vmem_limit_bytes=LARGE),
        name="encode_and_decode_away",
    )(pos, enc, bias, dec, *rows)


def mine(pos, lat, dec, dec_bias, targets):
    return pl.pallas_call(
        mine_kernel,
        in_specs=[SM, VM, ANY, VM, VM],
        out_specs=(VM, VM),
        out_shape=(PARTIAL, jax.ShapeDtypeStruct((4, D), jnp.float32)),
        scratch_shapes=HELD + SEMS,
        cost_estimate=pl.CostEstimate(
            flops=4 * 2 * 256 * 256 * D, bytes_accessed=10 * 2**20, transcendentals=0
        ),
        compiler_params=pltpu.CompilerParams(vmem_limit_bytes=LARGE),
        name="decode_mine",
    )(pos, lat, dec, dec_bias, targets)


def grad_kernel(which, pos, lat, errs, *rest):
    out, held, sems = rest[-3:]
    owner = pos[0]
    core = pos[1] if which == 0 else 1 - pos[1]
    place = pos[3 + which]
    writes = []
    for zh in range(2):
        first = 2 * (2 * zh + core)
        slots = decoder_slots(zh, core, owner)
        for h in range(2):
            copies = []
            for tt in range(2):
                target, j = first + tt, 4 * zh + 2 * h + tt
                valid = (target >= owner) if h == 0 else (target + 1 >= LAYERS - owner)
                copy = pltpu.make_async_copy(held.at[j], out.at[slots[2 * h + tt]], sems.at[j])
                copies.append((valid, copy))
            writes += copies

            @pl.when(copies[1][0])
            def _():
                lhs = jnp.concatenate([lat[which, h, 0], lat[which, h, 1]], axis=1)
                for d in range(0, D, DC):
                    rows = [
                        errs[(place + k) % 4, :, zh, :, d : d + DC].reshape(64, DC) for k in range(4)
                    ]
                    total = lax.dot_general(
                        lhs,
                        jnp.concatenate(rows, axis=0),
                        (((0,), (0,)), ((), ())),
                        preferred_element_type=jnp.float32,
                    )
                    total = (total * (BLK**-0.5)).astype(jnp.bfloat16).reshape(2, BLK, DC)
                    held[4 * zh + 2 * h : 4 * zh + 2 * h + 2, :, d : d + DC] = total
                for valid, copy in copies:
                    pl.when(valid)(copy.start)

    for valid, copy in writes:
        pl.when(valid)(copy.wait)


def gradients(which, pos, lat, errs, *before):
    return pl.pallas_call(
        functools.partial(grad_kernel, which),
        in_specs=[SM, VM, VM] + [ANY] * len(before),
        out_specs=ANY,
        out_shape=jax.ShapeDtypeStruct((PAIRS, BLK, D), jnp.bfloat16),
        scratch_shapes=HELD + SEMS,
        input_output_aliases={3: 0} if before else {},
        cost_estimate=pl.CostEstimate(
            flops=4 * 2 * 256 * 256 * D, bytes_accessed=8 * 2**20, transcendentals=0
        ),
        compiler_params=pltpu.CompilerParams(vmem_limit_bytes=VMEM),
        name="gradients",
    )(pos, lat, errs, *before)


ALL = ("zh", "co", "zl", "x", "y")


def lines(wide):
    groups = []
    for outer in range(16):
        for other in range(4):
            along_x = (outer // 4 % 2 == 0) == wide
            groups.append(
                [outer * 16 + (k * 4 + other if along_x else other * 4 + k) for k in range(4)]
            )
    return groups


def shift(block, groups, k):
    perm = [(line[i], line[(i + k) % 4]) for line in groups for i in range(4)]
    return lax.ppermute(block, ALL, perm)


def gather4(block, groups):
    return [block] + [shift(block, groups, -k) for k in (1, 2, 3)]


def reduce4(pieces, groups):
    total = pieces[0].astype(jnp.float32)
    for k in (1, 2, 3):
        total = total + shift(pieces[k], groups, k).astype(jnp.float32)
    return total


def local(resid_in, enc_weight, enc_bias, dec_weight, dec_bias, act_blocks, tile_order, targets):
    core, x, y = lax.axis_index("co"), lax.axis_index("x"), lax.axis_index("y")
    at_wide, at_narrow = jnp.where(core == 0, x, y), jnp.where(core == 0, y, x)
    pos = [lax.axis_index(LAYER), core, lax.axis_index("zl"), at_wide, at_narrow]
    listed = jnp.any(act_blocks[:, 0] == lax.axis_index(LAT), axis=2)
    hits = jnp.where(tile_order[None] == 0, listed[:, :1], listed[:, 1:])
    pos = jnp.concatenate([jnp.stack(pos).astype(jnp.int32), hits.reshape(4).astype(jnp.int32)])
    swap = [(0, 1), (1, 0)]
    wide, narrow = lines(True), lines(False)
    z_lines = [[o // 16 * 64 + k * 16 + o % 16 for k in range(4)] for o in range(64)]
    rows = jnp.concatenate(gather4(resid_in.reshape(4, D), z_lines))
    rows = gather4(jnp.concatenate(gather4(rows, narrow)), wide)
    bias = enc_bias[:, 0].astype(jnp.float32)
    lat, sent = away(pos, enc_weight[:, 0], bias, dec_weight[0], rows)
    received = lax.ppermute(sent.astype(jnp.float16), "co", swap)
    partial, base = mine(pos, lat, dec_weight[0], dec_bias, targets)
    partial = (partial + received.astype(jnp.float32)).astype(jnp.float16).reshape(4, 128, D)
    partial = reduce4([partial[k] for k in range(4)], wide).astype(jnp.float16).reshape(4, 32, D)
    column = reduce4([partial[k] for k in range(4)], narrow).astype(jnp.float16).reshape(8, 4, D)
    column = lax.all_to_all(column, Z, 0, 0, tiled=True).astype(jnp.float32)
    errs = (jnp.sum(column, axis=0) * (1.0 / SEND) + base).astype(jnp.bfloat16)
    recon_error = errs.reshape(2, 2, D)
    errs = lax.all_to_all(jnp.broadcast_to(errs[None], (8, 4, D)), Z, 0, 0, tiled=True)
    errs = jnp.concatenate(gather4(errs.reshape(32, D), narrow))
    own = jnp.broadcast_to(errs[None], (4, 128, D))
    own = lax.all_to_all(own, ALL, 0, 0, axis_index_groups=wide, tiled=True).reshape(4, 4, 2, 16, D)
    other = lax.ppermute(own, "co", swap)
    dec_grad = gradients(0, pos, lat, own)
    dec_grad = gradients(1, pos, lat, other, dec_grad)
    return (recon_error, dec_grad[None])


def solution(mesh):
    fine = Mesh(mesh.devices.reshape(2, 2, 4, 4, 4), ALL)
    return jax.shard_map(
        local,
        mesh=fine,
        in_specs=(
            P(LAT, None, LAYER, None),
            P(None, LAYER, None, LAT),
            P(None, LAYER, LAT),
            P(LAYER, None, LAT, None),
            P(LAYER, None),
            P(None, LAYER, None, None),
            P(),
            P(LAT, LAYER, None),
        ),
        out_specs=(P(LAT, LAYER, None), P(LAYER, None, LAT, None)),
        check_vma=False,
    )
```

```python
import functools

import jax
import jax.numpy as jnp
from jax import lax
from jax.experimental import pallas as pl
from jax.experimental.pallas import tpu as pltpu
from jax.sharding import Mesh
from jax.sharding import PartitionSpec as P

BLK = 128
D = 2304
DC = 768
PAIRS = 9
LAYERS = 8
SEND = 2.0**-5
VMEM = 14 * 1024 * 1024
LARGE = 44 * 1024 * 1024
LAT = ("zl", "x", "y")
LAYER = ("zh", "co")


def product(zh, core, owner, lat, weight, put):
    first = 2 * (2 * zh + core)
    late = first + 2 >= LAYERS - owner

    def halves(count):
        left = []
        for h in range(count):
            cols = []
            for tt in range(2):
                target = first + tt
                valid = (target >= owner) if h == 0 else (target + 1 >= LAYERS - owner)
                cols.append(lat[h, tt] * valid.astype(jnp.bfloat16))
            left.append(jnp.concatenate(cols, axis=1))
        for d in range(0, D, DC):
            total = jnp.zeros((256, DC), jnp.float32)
            for h in range(count):
                right = [weight[4 * zh + 2 * h + tt, :, d : d + DC] for tt in range(2)]
                total += jnp.dot(
                    left[h], jnp.concatenate(right, axis=0), preferred_element_type=jnp.float32
                )
            put(d, (total * SEND).reshape(16, 16, DC))

    pl.when(late)(lambda: halves(2))
    pl.when(jnp.logical_not(late))(lambda: halves(1))


def decoder_slots(zh, core, owner):
    slots = []
    for h in range(2):
        for tt in range(2):
            target = 2 * (2 * zh + core) + tt
            if h == 0:
                slots.append(jnp.maximum(target - owner, 0))
            else:
                slots.append(jnp.maximum(target + 1, LAYERS - owner))
    return slots


def fetch(zh, core, owner, weight, held, sems):
    copies = []
    for j, slot in enumerate(decoder_slots(zh, core, owner)):
        j += 4 * zh
        copies.append(pltpu.make_async_copy(weight.at[slot], held.at[j], sems.at[j]))
    return copies


def decode_pairs(core, owner, lat, held, copies, out):
    for zh in range(2):
        for copy in copies[zh]:
            copy.wait()

        def put(d, block):
            out[:, zh, :, d : d + DC] = block

        product(zh, core, owner, lat, held, put)


def away_kernel(pos, enc, bias, dec, g0, g1, g2, g3, lat, out, enc_held, held, enc_sems, sems):
    owner, core, zl = (pos[j] for j in range(3))
    enc_copies = [pltpu.make_async_copy(enc.at[h], enc_held.at[h], enc_sems.at[h]) for h in range(2)]
    dec_copies = [fetch(zh, 1 - core, owner, dec, held, sems) for zh in range(2)]
    for copy in enc_copies + dec_copies[0] + dec_copies[1]:
        copy.start()
    g = jnp.concatenate([g0[...], g1[...], g2[...], g3[...]], axis=0)
    tile_row = (lax.broadcasted_iota(jnp.int32, (256, BLK), 0) // 4 + zl) % 4 // 2
    q = lax.broadcasted_iota(jnp.int32, (256, 256), 0)
    c = lax.broadcasted_iota(jnp.int32, (256, 256), 1)
    same = (q // 4 % 4 == c // 4 % 4) & (q // 2 % 2 == c // 2 % 2)
    own = same & (q // 16 == c // 16)
    other = same & (c // 64 == q // 16 % 4) & (c // 16 % 4 == q // 64)
    for h in range(2):
        enc_copies[h].wait()
        pre = jnp.dot(g, enc_held[h], preferred_element_type=jnp.float32)
        pre = pre + bias[h : h + 1]
        on = jnp.where(tile_row == 0, pos[5 + 2 * h], pos[6 + 2 * h]) > 0
        value = jnp.where(on, jnp.maximum(pre, 0.0), 0.0).astype(jnp.bfloat16)
        for tt in range(2):
            half = (q % 2 == tt) & (c % 2 == h)
            for which, place in enumerate((own, other)):
                lat[which, h, tt] = jnp.dot(
                    (place & half).astype(jnp.bfloat16), value, preferred_element_type=jnp.float32
                ).astype(jnp.bfloat16)
    decode_pairs(1 - core, owner, lat.at[1], held, dec_copies, out)


def mine_kernel(pos, lat, dec, dec_bias, targets, out, base, held, sems):
    owner, core = pos[0], pos[1]
    copies = [fetch(zh, core, owner, dec, held, sems) for zh in range(2)]
    for copy in copies[0] + copies[1]:
        copy.start()
    for r in range(2):
        for tt in range(2):
            row = dec_bias[tt : tt + 1].astype(jnp.float32) - targets[r, tt : tt + 1].astype(jnp.float32)
            base[2 * r + tt : 2 * r + tt + 1] = row
    decode_pairs(core, owner, lat.at[0], held, copies, out)


SM = pl.BlockSpec(memory_space=pltpu.SMEM)
VM = pl.BlockSpec(memory_space=pltpu.VMEM)
ANY = pl.BlockSpec(memory_space=pltpu.HBM)
PARTIAL = jax.ShapeDtypeStruct((16, 2, 16, D), jnp.float32)


HELD = [pltpu.VMEM((8, BLK, D), jnp.bfloat16)]
SEMS = [pltpu.SemaphoreType.DMA((8,))]


def away(pos, enc, bias, dec, rows):
    return pl.pallas_call(
        away_kernel,
        in_specs=[SM, ANY, VM, ANY, VM, VM, VM, VM],
        out_specs=(VM, VM),
        out_shape=(jax.ShapeDtypeStruct((2, 2, 2, 256, BLK), jnp.bfloat16), PARTIAL),
        scratch_shapes=[pltpu.VMEM((2, D, BLK), jnp.bfloat16)]
        + HELD
        + [pltpu.SemaphoreType.DMA((2,))]
        + SEMS,
        cost_estimate=pl.CostEstimate(
            flops=6 * 2 * 256 * 256 * D, bytes_accessed=12 * 2**20, transcendentals=0
        ),
        compiler_params=pltpu.CompilerParams(vmem_limit_bytes=LARGE),
        name="encode_and_decode_away",
    )(pos, enc, bias, dec, *rows)


def mine(pos, lat, dec, dec_bias, targets):
    return pl.pallas_call(
        mine_kernel,
        in_specs=[SM, VM, ANY, VM, VM],
        out_specs=(VM, VM),
        out_shape=(PARTIAL, jax.ShapeDtypeStruct((4, D), jnp.float32)),
        scratch_shapes=HELD + SEMS,
        cost_estimate=pl.CostEstimate(
            flops=4 * 2 * 256 * 256 * D, bytes_accessed=10 * 2**20, transcendentals=0
        ),
        compiler_params=pltpu.CompilerParams(vmem_limit_bytes=LARGE),
        name="decode_mine",
    )(pos, lat, dec, dec_bias, targets)


def grad_kernel(which, pos, lat, errs, *rest):
    out, held, sems = rest[-3:]
    owner = pos[0]
    core = pos[1] if which == 0 else 1 - pos[1]
    place = pos[3 + which]
    writes = []
    for zh in range(2):
        first = 2 * (2 * zh + core)
        slots = decoder_slots(zh, core, owner)
        for h in range(2):
            copies = []
            for tt in range(2):
                target, j = first + tt, 4 * zh + 2 * h + tt
                valid = (target >= owner) if h == 0 else (target + 1 >= LAYERS - owner)
                copy = pltpu.make_async_copy(held.at[j], out.at[slots[2 * h + tt]], sems.at[j])
                copies.append((valid, copy))
            writes += copies

            @pl.when(copies[1][0])
            def _():
                lhs = jnp.concatenate([lat[which, h, 0], lat[which, h, 1]], axis=1)
                for d in range(0, D, DC):
                    rows = [
                        errs[(place + k) % 4, :, zh, :, d : d + DC].reshape(64, DC) for k in range(4)
                    ]
                    total = lax.dot_general(
                        lhs,
                        jnp.concatenate(rows, axis=0),
                        (((0,), (0,)), ((), ())),
                        preferred_element_type=jnp.float32,
                    )
                    total = (total * (BLK**-0.5)).astype(jnp.bfloat16).reshape(2, BLK, DC)
                    held[4 * zh + 2 * h : 4 * zh + 2 * h + 2, :, d : d + DC] = total
                for valid, copy in copies:
                    pl.when(valid)(copy.start)

    for valid, copy in writes:
        pl.when(valid)(copy.wait)


def gradients(which, pos, lat, errs, *before):
    return pl.pallas_call(
        functools.partial(grad_kernel, which),
        in_specs=[SM, VM, VM] + [ANY] * len(before),
        out_specs=ANY,
        out_shape=jax.ShapeDtypeStruct((PAIRS, BLK, D), jnp.bfloat16),
        scratch_shapes=HELD + SEMS,
        input_output_aliases={3: 0} if before else {},
        cost_estimate=pl.CostEstimate(
            flops=4 * 2 * 256 * 256 * D, bytes_accessed=8 * 2**20, transcendentals=0
        ),
        compiler_params=pltpu.CompilerParams(vmem_limit_bytes=VMEM),
        name="gradients",
    )(pos, lat, errs, *before)


ALL = ("zh", "co", "zl", "x", "y")


def lines(wide):
    groups = []
    for outer in range(16):
        for other in range(4):
            along_x = (outer // 4 % 2 == 0) == wide
            groups.append(
                [outer * 16 + (k * 4 + other if along_x else other * 4 + k) for k in range(4)]
            )
    return groups


def shift(block, groups, k):
    perm = [(line[i], line[(i + k) % 4]) for line in groups for i in range(4)]
    return lax.ppermute(block, ALL, perm)


def gather4(block, groups):
    return [block] + [shift(block, groups, -k) for k in (1, 2, 3)]


def reduce4(pieces, groups):
    total = pieces[0].astype(jnp.float32)
    for k in (1, 2, 3):
        total = total + shift(pieces[k], groups, k).astype(jnp.float32)
    return total


def local(resid_in, enc_weight, enc_bias, dec_weight, dec_bias, act_blocks, tile_order, targets):
    core, x, y = lax.axis_index("co"), lax.axis_index("x"), lax.axis_index("y")
    at_wide, at_narrow = jnp.where(core == 0, x, y), jnp.where(core == 0, y, x)
    pos = [lax.axis_index(LAYER), core, lax.axis_index("zl"), at_wide, at_narrow]
    listed = jnp.any(act_blocks[:, 0] == lax.axis_index(LAT), axis=2)
    hits = jnp.where(tile_order[None] == 0, listed[:, :1], listed[:, 1:])
    pos = jnp.concatenate([jnp.stack(pos).astype(jnp.int32), hits.reshape(4).astype(jnp.int32)])
    swap = [(0, 1), (1, 0)]
    wide, narrow = lines(True), lines(False)
    z_lines = [[o // 16 * 64 + k * 16 + o % 16 for k in range(4)] for o in range(64)]
    rows = jnp.concatenate(gather4(resid_in.reshape(4, D), z_lines))
    rows = gather4(jnp.concatenate(gather4(rows, narrow)), wide)
    bias = enc_bias[:, 0].astype(jnp.float32)
    lat, sent = away(pos, enc_weight[:, 0], bias, dec_weight[0], rows)
    received = lax.ppermute(sent.astype(jnp.float16), "co", swap)
    partial, base = mine(pos, lat, dec_weight[0], dec_bias, targets)
    partial = (partial + received.astype(jnp.float32)).astype(jnp.float16).reshape(4, 128, D)
    partial = reduce4([partial[k] for k in range(4)], wide).astype(jnp.float16).reshape(4, 32, D)
    column = reduce4([partial[k] for k in range(4)], narrow).astype(jnp.float16).reshape(2, 4, 4, D)
    column = reduce4([column[:, k] for k in range(4)], z_lines)
    at_half = jnp.arange(2)[:, None, None] == lax.axis_index("zh")
    column = (column + jnp.where(at_half, base[None] * SEND, 0.0)).astype(jnp.float16)
    far = lax.ppermute(column, "zh", swap)
    errs = ((column.astype(jnp.float32) + far.astype(jnp.float32)) * (1.0 / SEND)).astype(jnp.bfloat16)
    recon_error = jnp.where(lax.axis_index("zh") == 0, errs[0], errs[1]).reshape(2, 2, D)
    errs = jnp.stack(gather4(errs, z_lines), axis=1).reshape(32, D)
    errs = jnp.concatenate(gather4(errs, narrow))
    own = jnp.broadcast_to(errs[None], (4, 128, D))
    own = lax.all_to_all(own, ALL, 0, 0, axis_index_groups=wide, tiled=True).reshape(4, 4, 2, 16, D)
    other = lax.ppermute(own, "co", swap)
    dec_grad = gradients(0, pos, lat, own)
    dec_grad = gradients(1, pos, lat, other, dec_grad)
    return (recon_error, dec_grad[None])


def solution(mesh):
    fine = Mesh(mesh.devices.reshape(2, 2, 4, 4, 4), ALL)
    return jax.shard_map(
        local,
        mesh=fine,
        in_specs=(
            P(LAT, None, LAYER, None),
            P(None, LAYER, None, LAT),
            P(None, LAYER, LAT),
            P(LAYER, None, LAT, None),
            P(LAYER, None),
            P(None, LAYER, None, None),
            P(),
            P(LAT, LAYER, None),
        ),
        out_specs=(P(LAT, LAYER, None), P(LAYER, None, LAT, None)),
        check_vma=False,
    )
```

```python
import functools

import jax
import jax.numpy as jnp
from jax import lax
from jax.experimental import pallas as pl
from jax.experimental.pallas import tpu as pltpu
from jax.sharding import Mesh
from jax.sharding import PartitionSpec as P

BLK = 128
D = 2304
DC = 768
PAIRS = 9
LAYERS = 8
SEND = 2.0**-5
VMEM = 14 * 1024 * 1024
LARGE = 44 * 1024 * 1024
LAT = ("zl", "x", "y")
LAYER = ("zh", "co")


def product(zh, core, owner, lat, weight, put):
    first = 2 * (2 * zh + core)
    late = first + 2 >= LAYERS - owner

    def halves(count):
        left = []
        for h in range(count):
            cols = []
            for tt in range(2):
                target = first + tt
                valid = (target >= owner) if h == 0 else (target + 1 >= LAYERS - owner)
                cols.append(lat[h, tt] * valid.astype(jnp.bfloat16))
            left.append(jnp.concatenate(cols, axis=1))
        for d in range(0, D, DC):
            total = jnp.zeros((256, DC), jnp.float32)
            for h in range(count):
                right = [weight[4 * zh + 2 * h + tt, :, d : d + DC] for tt in range(2)]
                total += jnp.dot(
                    left[h], jnp.concatenate(right, axis=0), preferred_element_type=jnp.float32
                )
            put(d, (total * SEND).reshape(16, 16, DC))

    pl.when(late)(lambda: halves(2))
    pl.when(jnp.logical_not(late))(lambda: halves(1))


def decoder_slots(zh, core, owner):
    slots = []
    for h in range(2):
        for tt in range(2):
            target = 2 * (2 * zh + core) + tt
            if h == 0:
                slots.append(jnp.maximum(target - owner, 0))
            else:
                slots.append(jnp.maximum(target + 1, LAYERS - owner))
    return slots


def fetch(zh, core, owner, weight, held, sems):
    copies = []
    for j, slot in enumerate(decoder_slots(zh, core, owner)):
        j += 4 * zh
        copies.append(pltpu.make_async_copy(weight.at[slot], held.at[j], sems.at[j]))
    return copies


def decode_pairs(core, owner, lat, held, copies, out):
    for zh in range(2):
        for copy in copies[zh]:
            copy.wait()

        def put(d, block):
            out[:, zh, :, d : d + DC] = block

        product(zh, core, owner, lat, held, put)


def away_kernel(pos, enc, bias, dec, g0, g1, g2, g3, lat, out, enc_held, held, enc_sems, sems):
    owner, core, zl = (pos[j] for j in range(3))
    enc_copies = [pltpu.make_async_copy(enc.at[h], enc_held.at[h], enc_sems.at[h]) for h in range(2)]
    dec_copies = [fetch(zh, 1 - core, owner, dec, held, sems) for zh in range(2)]
    for copy in enc_copies + dec_copies[0] + dec_copies[1]:
        copy.start()
    g = jnp.concatenate([g0[...], g1[...], g2[...], g3[...]], axis=0)
    tile_row = (lax.broadcasted_iota(jnp.int32, (256, BLK), 0) // 4 + zl) % 4 // 2
    q = lax.broadcasted_iota(jnp.int32, (256, 256), 0)
    c = lax.broadcasted_iota(jnp.int32, (256, 256), 1)
    same = (q // 4 % 4 == c // 4 % 4) & (q // 2 % 2 == c // 2 % 2)
    own = same & (q // 16 == c // 16)
    other = same & (c // 64 == q // 16 % 4) & (c // 16 % 4 == q // 64)
    for h in range(2):
        enc_copies[h].wait()
        pre = jnp.dot(g, enc_held[h], preferred_element_type=jnp.float32)
        pre = pre + bias[h : h + 1]
        on = jnp.where(tile_row == 0, pos[5 + 2 * h], pos[6 + 2 * h]) > 0
        value = jnp.where(on, jnp.maximum(pre, 0.0), 0.0).astype(jnp.bfloat16)
        for tt in range(2):
            half = (q % 2 == tt) & (c % 2 == h)
            for which, place in enumerate((own, other)):
                lat[which, h, tt] = jnp.dot(
                    (place & half).astype(jnp.bfloat16), value, preferred_element_type=jnp.float32
                ).astype(jnp.bfloat16)
    decode_pairs(1 - core, owner, lat.at[1], held, dec_copies, out)


def mine_kernel(pos, lat, dec, dec_bias, targets, out, base, held, sems):
    owner, core = pos[0], pos[1]
    copies = [fetch(zh, core, owner, dec, held, sems) for zh in range(2)]
    for copy in copies[0] + copies[1]:
        copy.start()
    for r in range(2):
        for tt in range(2):
            row = dec_bias[tt : tt + 1].astype(jnp.float32) - targets[r, tt : tt + 1].astype(jnp.float32)
            base[2 * r + tt : 2 * r + tt + 1] = row
    decode_pairs(core, owner, lat.at[0], held, copies, out)


SM = pl.BlockSpec(memory_space=pltpu.SMEM)
VM = pl.BlockSpec(memory_space=pltpu.VMEM)
ANY = pl.BlockSpec(memory_space=pltpu.HBM)
PARTIAL = jax.ShapeDtypeStruct((16, 2, 16, D), jnp.float32)


HELD = [pltpu.VMEM((8, BLK, D), jnp.bfloat16)]
SEMS = [pltpu.SemaphoreType.DMA((8,))]
FAR = [pltpu.VMEM((2, 4, 4, 16, D), jnp.bfloat16), pltpu.SemaphoreType.DMA((2,))]


def away(pos, enc, bias, dec, rows):
    return pl.pallas_call(
        away_kernel,
        in_specs=[SM, ANY, VM, ANY, VM, VM, VM, VM],
        out_specs=(VM, VM),
        out_shape=(jax.ShapeDtypeStruct((2, 2, 2, 256, BLK), jnp.bfloat16), PARTIAL),
        scratch_shapes=[pltpu.VMEM((2, D, BLK), jnp.bfloat16)]
        + HELD
        + [pltpu.SemaphoreType.DMA((2,))]
        + SEMS,
        cost_estimate=pl.CostEstimate(
            flops=6 * 2 * 256 * 256 * D, bytes_accessed=12 * 2**20, transcendentals=0
        ),
        compiler_params=pltpu.CompilerParams(vmem_limit_bytes=LARGE),
        name="encode_and_decode_away",
    )(pos, enc, bias, dec, *rows)


def mine(pos, lat, dec, dec_bias, targets):
    return pl.pallas_call(
        mine_kernel,
        in_specs=[SM, VM, ANY, VM, VM],
        out_specs=(VM, VM),
        out_shape=(PARTIAL, jax.ShapeDtypeStruct((4, D), jnp.float32)),
        scratch_shapes=HELD + SEMS,
        cost_estimate=pl.CostEstimate(
            flops=4 * 2 * 256 * 256 * D, bytes_accessed=10 * 2**20, transcendentals=0
        ),
        compiler_params=pltpu.CompilerParams(vmem_limit_bytes=LARGE),
        name="decode_mine",
    )(pos, lat, dec, dec_bias, targets)


def grad_kernel(which, pos, lat, errs, *rest):
    if which == 0:
        out, held, sems = rest
        halves = [errs.at[:, :, zh] for zh in range(2)]
    else:
        out, held, sems, halves, in_sems = rest[1:]
        reads = [pltpu.make_async_copy(errs.at[:, :, zh], halves.at[zh], in_sems.at[zh]) for zh in range(2)]
        for read in reads:
            read.start()
        halves = [halves.at[zh] for zh in range(2)]
    owner = pos[0]
    core = pos[1] if which == 0 else 1 - pos[1]
    place = pos[3 + which]
    writes = []
    for zh in range(2):
        if which == 1:
            reads[zh].wait()
        first = 2 * (2 * zh + core)
        slots = decoder_slots(zh, core, owner)
        for h in range(2):
            copies = []
            for tt in range(2):
                target, j = first + tt, 4 * zh + 2 * h + tt
                valid = (target >= owner) if h == 0 else (target + 1 >= LAYERS - owner)
                copy = pltpu.make_async_copy(held.at[j], out.at[slots[2 * h + tt]], sems.at[j])
                copies.append((valid, copy))
            writes += copies

            @pl.when(copies[1][0])
            def _():
                lhs = jnp.concatenate([lat[which, h, 0], lat[which, h, 1]], axis=1)
                for d in range(0, D, DC):
                    rows = [
                        halves[zh][(place + k) % 4, :, :, d : d + DC].reshape(64, DC) for k in range(4)
                    ]
                    total = lax.dot_general(
                        lhs,
                        jnp.concatenate(rows, axis=0),
                        (((0,), (0,)), ((), ())),
                        preferred_element_type=jnp.float32,
                    )
                    total = (total * (BLK**-0.5)).astype(jnp.bfloat16).reshape(2, BLK, DC)
                    held[4 * zh + 2 * h : 4 * zh + 2 * h + 2, :, d : d + DC] = total
                for valid, copy in copies:
                    pl.when(valid)(copy.start)

    for valid, copy in writes:
        pl.when(valid)(copy.wait)


def gradients(which, pos, lat, errs, *before):
    return pl.pallas_call(
        functools.partial(grad_kernel, which),
        in_specs=[SM, VM, ANY if before else VM] + [ANY] * len(before),
        out_specs=ANY,
        out_shape=jax.ShapeDtypeStruct((PAIRS, BLK, D), jnp.bfloat16),
        scratch_shapes=HELD + SEMS + (FAR if before else []),
        input_output_aliases={3: 0} if before else {},
        cost_estimate=pl.CostEstimate(
            flops=4 * 2 * 256 * 256 * D, bytes_accessed=8 * 2**20, transcendentals=0
        ),
        compiler_params=pltpu.CompilerParams(vmem_limit_bytes=VMEM),
        name="gradients",
    )(pos, lat, errs, *before)


ALL = ("zh", "co", "zl", "x", "y")


def lines(wide):
    groups = []
    for outer in range(16):
        for other in range(4):
            along_x = (outer // 4 % 2 == 0) == wide
            groups.append(
                [outer * 16 + (k * 4 + other if along_x else other * 4 + k) for k in range(4)]
            )
    return groups


def shift(block, groups, k):
    perm = [(line[i], line[(i + k) % 4]) for line in groups for i in range(4)]
    return lax.ppermute(block, ALL, perm)


def gather4(block, groups):
    return [block] + [shift(block, groups, -k) for k in (1, 2, 3)]


def reduce4(pieces, groups):
    total = pieces[0].astype(jnp.float32)
    for k in (1, 2, 3):
        total = total + shift(pieces[k], groups, k).astype(jnp.float32)
    return total


def local(resid_in, enc_weight, enc_bias, dec_weight, dec_bias, act_blocks, tile_order, targets):
    core, x, y = lax.axis_index("co"), lax.axis_index("x"), lax.axis_index("y")
    at_wide, at_narrow = jnp.where(core == 0, x, y), jnp.where(core == 0, y, x)
    pos = [lax.axis_index(LAYER), core, lax.axis_index("zl"), at_wide, at_narrow]
    listed = jnp.any(act_blocks[:, 0] == lax.axis_index(LAT), axis=2)
    hits = jnp.where(tile_order[None] == 0, listed[:, :1], listed[:, 1:])
    pos = jnp.concatenate([jnp.stack(pos).astype(jnp.int32), hits.reshape(4).astype(jnp.int32)])
    swap = [(0, 1), (1, 0)]
    wide, narrow = lines(True), lines(False)
    z_lines = [[o // 16 * 64 + k * 16 + o % 16 for k in range(4)] for o in range(64)]
    rows = jnp.concatenate(gather4(resid_in.reshape(4, D), z_lines))
    rows = gather4(jnp.concatenate(gather4(rows, narrow)), wide)
    bias = enc_bias[:, 0].astype(jnp.float32)
    lat, sent = away(pos, enc_weight[:, 0], bias, dec_weight[0], rows)
    received = lax.ppermute(sent.astype(jnp.float16), "co", swap)
    partial, base = mine(pos, lat, dec_weight[0], dec_bias, targets)
    partial = (partial + received.astype(jnp.float32)).astype(jnp.float16).reshape(4, 128, D)
    partial = reduce4([partial[k] for k in range(4)], wide).astype(jnp.float16).reshape(4, 32, D)
    column = reduce4([partial[k] for k in range(4)], narrow).astype(jnp.float16).reshape(2, 4, 4, D)
    column = reduce4([column[:, k] for k in range(4)], z_lines)
    at_half = jnp.arange(2)[:, None, None] == lax.axis_index("zh")
    column = (column + jnp.where(at_half, base[None] * SEND, 0.0)).astype(jnp.float16)
    far = lax.ppermute(column, "zh", swap)
    errs = ((column.astype(jnp.float32) + far.astype(jnp.float32)) * (1.0 / SEND)).astype(jnp.bfloat16)
    recon_error = jnp.where(lax.axis_index("zh") == 0, errs[0], errs[1]).reshape(2, 2, D)
    errs = jnp.stack(gather4(errs, z_lines), axis=1).reshape(32, D)
    errs = jnp.concatenate(gather4(errs, narrow))
    own = jnp.broadcast_to(errs[None], (4, 128, D))
    own = lax.all_to_all(own, ALL, 0, 0, axis_index_groups=wide, tiled=True).reshape(4, 4, 2, 16, D)
    other = lax.ppermute(own, "co", swap)
    dec_grad = gradients(0, pos, lat, own)
    dec_grad = gradients(1, pos, lat, other, dec_grad)
    return (recon_error, dec_grad[None])


def solution(mesh):
    fine = Mesh(mesh.devices.reshape(2, 2, 4, 4, 4), ALL)
    return jax.shard_map(
        local,
        mesh=fine,
        in_specs=(
            P(LAT, None, LAYER, None),
            P(None, LAYER, None, LAT),
            P(None, LAYER, LAT),
            P(LAYER, None, LAT, None),
            P(LAYER, None),
            P(None, LAYER, None, None),
            P(),
            P(LAT, LAYER, None),
        ),
        out_specs=(P(LAT, LAYER, None), P(LAYER, None, LAT, None)),
        check_vma=False,
    )
```
